32 devices in a mesh: tok: 4 (over z), hid: 8 (over y, x, core).
Axes of the slice: x: 2, y: 2, z: 4, core: 2. Of those that a mesh axis runs over, the one named last changes fastest.
Arguments:
- out_grad: bfloat16 [1024, 8192], P('hid', 'tok'), may hold values from -6 to 6
- gate_act: bfloat16 [1024, 28672], P('tok', 'hid'), may hold values from -8 to 8
- up_act: bfloat16 [1024, 28672], P('tok', 'hid'), may hold values from -6 to 6
- gate_weight: bfloat16 [8192, 28672], P('tok', 'hid'), may hold values from -0.0625 to 0.0625
- up_weight: bfloat16 [8192, 28672], P('tok', 'hid'), may hold values from -0.0625 to 0.0625
- down_weight: bfloat16 [28672, 8192], P('hid', 'tok'), may hold values from -0.03125 to 0.03125
Outputs:
- input_grad: bfloat16 [1024, 8192], P('hid', 'tok')
The draws below stay inside these ranges and needn't reach their ends.
All inputs are finite; a program needn't handle non-finite values.
Results may differ from the reference program's by a relative error of at most 0.005.
Values may be sent and summed in bfloat16 or wider, within the bound.
A program may use at most 128 MiB of HBM per device.

```python
import jax
import jax.numpy as jnp
from jax import lax

D = 8192
FF = 28672
TOKENS = 1024
N_HID = 8


def steps_of(own_key, shape, cuts, low, largest):
    factor_of, own = 1.0, jax.random.fold_in(own_key, 6)
    for axis_at, shards_of in cuts:
        draws = jnp.exp(jax.random.uniform(jax.random.fold_in(own, axis_at), (shards_of,), jnp.float32, low / len(cuts), largest / len(cuts)))
        factor_of = factor_of * jnp.repeat(draws, shape[axis_at] // shards_of).reshape([-1 if axis == axis_at else 1 for axis in range(len(shape))])
    return factor_of


def scatter_about(stream_key, extent, deviation, most, pieces=(), kind=jnp.bfloat16):
    drawn = jax.random.normal(stream_key, extent, jnp.float32) * deviation
    if len(pieces) > 0:
        drawn = steps_of(stream_key, extent, pieces, -0.22, 0.18) * drawn
    return jnp.clip(drawn, min=-most, max=most).astype(kind)


def setup_inputs(seed: int = 0) -> dict:
    splits = jax.random.split(jax.random.key(seed), 7)
    out_grad = scatter_about(splits[0], (TOKENS, D), 1.0, 6.0, ((0, 8), (1, 4)))
    gate_act = scatter_about(splits[1], (TOKENS, FF), 1.5, 8.0, ((0, 4), (1, 8)))
    up_act = scatter_about(splits[2], (TOKENS, FF), 1.0, 6.0, ((0, 4), (1, 8)))
    gate_weight = scatter_about(splits[3], (D, FF), D ** -0.5, 0.0625, ((0, 4), (1, 8)))
    up_weight = scatter_about(splits[4], (D, FF), D ** -0.5, 0.0625, ((0, 4), (1, 8)))
    down_weight = scatter_about(splits[5], (FF, D), FF ** -0.5, 0.03125, ((0, 8), (1, 4)))
    return {"out_grad": out_grad, "gate_act": gate_act, "up_act": up_act, "gate_weight": gate_weight, "up_weight": up_weight, "down_weight": down_weight}


def sylvester(order):
    index = jnp.arange(order, dtype=jnp.int32)
    anded = index[:, None] & index[None, :]
    count = jnp.zeros((order, order), jnp.int32)
    for level in range(order.bit_length()):
        count = count + ((anded >> level) & 1)
    return (1 - 2 * (count % 2)).astype(jnp.float32) * (1.0 / (order ** 0.5))


def reference(out_grad, gate_act, up_act, gate_weight, up_weight, down_weight):
    rotated_grad = lax.dot_general(out_grad, down_weight, (((1,), (1,)), ((), ())), preferred_element_type=jnp.float32)
    shaped = rotated_grad.reshape(TOKENS, N_HID, FF // N_HID)
    hadamard = sylvester(N_HID)
    hidden_grad = jnp.einsum("st,ktc->ksc", hadamard, shaped, precision=lax.Precision.HIGHEST).reshape(TOKENS, FF)
    gate = gate_act.astype(jnp.float32)
    upper = up_act.astype(jnp.float32)
    logistic = jax.nn.sigmoid(gate)
    gate_grad = (hidden_grad * upper * logistic * (1.0 + gate * (1.0 - logistic))).astype(jnp.bfloat16)
    up_grad = (hidden_grad * gate * logistic).astype(jnp.bfloat16)
    total = lax.dot_general(gate_grad, gate_weight, (((1,), (1,)), ((), ())), preferred_element_type=jnp.float32)
    total = total + lax.dot_general(up_grad, up_weight, (((1,), (1,)), ((), ())), preferred_element_type=jnp.float32)
    return total.astype(jnp.bfloat16)
```

```python
import math

import jax
import jax.numpy as jnp
from jax import lax
from jax.sharding import PartitionSpec as P

CHUNKS = 4


def swapped(x, axis, bit):
    return lax.ppermute(x, axis, [(i, i ^ 1 << bit) for i in range(lax.axis_size(axis))])


def contract_rows(left, right):
    return lax.dot_general(
        left, right, (((1,), (1,)), ((), ())), preferred_element_type=jnp.float32
    )


def body(out_grad, gate_act, up_act, gate_weight, up_weight, down_weight):
    hid_count = lax.axis_size("hid")
    position = lax.axis_index("hid")
    gathered = lax.all_gather(out_grad, "hid", axis=0, tiled=True)
    width = down_weight.shape[0] // CHUNKS
    total = None
    for chunk in range(CHUNKS):
        cut = slice(chunk * width, (chunk + 1) * width)
        product = contract_rows(gathered, down_weight[cut]).astype(jnp.bfloat16)
        current = lax.psum_scatter(product, "tok", scatter_dimension=0, tiled=True)
        current = current.astype(jnp.float32)
        for level in range(hid_count.bit_length() - 1):
            sent = current if level == 0 else current.astype(jnp.bfloat16)
            partner = swapped(sent, "hid", level).astype(jnp.float32)
            upper_half = position >> level & 1 == 1
            current = jnp.where(upper_half, partner - current, current + partner)
        hidden_grad = current * (1.0 / math.sqrt(hid_count))
        gate = gate_act[:, cut].astype(jnp.float32)
        upper = up_act[:, cut].astype(jnp.float32)
        logistic = jax.nn.sigmoid(gate)
        gate_grad = (hidden_grad * upper * logistic * (1.0 + gate * (1.0 - logistic))).astype(
            jnp.bfloat16
        )
        up_grad = (hidden_grad * gate * logistic).astype(jnp.bfloat16)
        both = jnp.concatenate([gate_grad, up_grad], axis=1)
        both = lax.all_gather(both, "tok", axis=0, tiled=True)
        part = contract_rows(both[:, :width], gate_weight[:, cut]) + contract_rows(
            both[:, width:], up_weight[:, cut]
        )
        total = part if total is None else total + part
    summed = lax.psum_scatter(total, "hid", scatter_dimension=0, tiled=True)
    return summed.astype(jnp.bfloat16)


def solution(mesh):
    in_specs = (
        P("hid", "tok"),
        P("tok", "hid"),
        P("tok", "hid"),
        P("tok", "hid"),
        P("tok", "hid"),
        P("hid", "tok"),
    )
    out_specs = P("hid", "tok")
    return jax.shard_map(body, mesh=mesh, in_specs=in_specs, out_specs=out_specs, check_vma=False)
```

```python
import functools
import math

import jax
import jax.numpy as jnp
from jax import lax
from jax.experimental import pallas as pl
from jax.experimental.pallas import tpu as pltpu
from jax.sharding import PartitionSpec as P

BF16, F32 = jnp.bfloat16, jnp.float32
MESH = pl.DeviceIdType.MESH


def dot_rows(left, right):
    return lax.dot_general(left, right, (((1,), (1,)), ((), ())), preferred_element_type=F32)


def kernel(
    Z, L, N, w, rows,
    x_ref, ga_ref, ua_ref, gw_hbm, uw_hbm, dw_hbm, acc,
    part, rs, mix0, mixn, cur, msend, grads, dwb, wb,
    rs_send, rs_recv, mix_send, mix_recv, ag_up, ag_dn, ag_recv, dw_sem, gw_sem, uw_sem,
):
    z = lax.axis_index("tok")
    hid = lax.axis_index("hid")
    last = Z - 1
    half = rows // 2
    base = last + L
    steps = N + base + last
    order = [list(range(L)), [0] + list(range(L - 1, 0, -1))]

    def bit_of(bit):
        return (hid // (1 << bit)) % 2

    def partner_of(bit):
        return hid + (1 - 2 * bit_of(bit)) * (1 << bit)

    def remote(src, dst, send, recv, **where):
        return pltpu.make_async_remote_copy(
            src_ref=src, dst_ref=dst, send_sem=send, recv_sem=recv,
            device_id=where, device_id_type=MESH,
        )

    def rs_copy(c, slot, to):
        return remote(rs.at[c, slot], rs.at[c, slot], rs_send.at[c, slot], rs_recv.at[c, slot], tok=to)

    def mix_copy(c, l, h):
        at = pl.ds(h * half, half)
        to = partner_of(order[h][l])
        if l == 0:
            src, dst = cur.at[0, at], mix0.at[c, at]
        else:
            src, dst = msend.at[l - 1, at], mixn.at[c, l - 1, at]
        return remote(src, dst, mix_send.at[l, h], mix_recv.at[c, l, h], hid=to)

    def ag_copy(c, b, to, sems):
        return remote(grads.at[c, b], grads.at[c, b], sems.at[c, b], ag_recv.at[c, b], tok=to)

    def dw_fetch(c):
        return pltpu.make_async_copy(
            dw_hbm.at[pl.ds(pl.multiple_of(c * w, w), w)], dwb.at[c % 2], dw_sem.at[c % 2])

    def gw_fetch(c):
        at = pl.ds(pl.multiple_of(c * w, w), w)
        return pltpu.make_async_copy(gw_hbm.at[:, at], wb.at[c % 2, :, pl.ds(0, w)], gw_sem.at[c % 2])

    def uw_fetch(c):
        at = pl.ds(pl.multiple_of(c * w, w), w)
        return pltpu.make_async_copy(uw_hbm.at[:, at], wb.at[c % 2, :, pl.ds(w, w)], uw_sem.at[c % 2])

    def within(c):
        return (c >= 0) & (c < N)

    def product(c):
        dw_fetch(c).wait()

        @pl.loop(0, Z)
        def _(b):
            at = pl.ds(pl.multiple_of(b * rows, rows), rows)
            part[c % Z, b] = dot_rows(x_ref[at, :], dwb[c % 2])

    barrier = pltpu.get_barrier_semaphore()

    @pl.when(z > 0)
    def _():
        pl.semaphore_signal(barrier, inc=1, device_id={"tok": z - 1}, device_id_type=MESH)

    @pl.when(z < last)
    def _():
        pl.semaphore_signal(barrier, inc=1, device_id={"tok": z + 1}, device_id_type=MESH)

    for bit in range(L):
        pl.semaphore_signal(barrier, inc=1, device_id={"hid": partner_of(bit)}, device_id_type=MESH)
    dw_fetch(0).start()
    dw_fetch(1).start()
    gw_fetch(0).start()
    uw_fetch(0).start()
    acc[...] = jnp.zeros_like(acc)
    pl.semaphore_wait(barrier, L + jnp.where(z > 0, 1, 0) + jnp.where(z < last, 1, 0))

    product(0)

    def combined(c, l):
        halves = []
        for h in (0, 1):
            copy = mix_copy(c, l, h)
            copy.wait_send()
            copy.wait_recv()
            at = pl.ds(h * half, half)
            got = mix0[c, at, :] if l == 0 else mixn[c, l - 1, at, :].astype(F32)
            sign = jnp.where(bit_of(order[h][l]) == 1, -1.0, 1.0).astype(F32)
            halves.append(cur[l, at, :] * sign + got)
        return halves

    @pl.loop(0, steps)
    def _(t):
        for k in range(last, 0, -1):
            c = t - base - k

            @pl.when(within(c) & (z - k >= 0))
            def _():
                b = z - k
                ag_copy(c, b, z, ag_up).wait_recv()

                @pl.when(z < last)
                def _():
                    ag_copy(c, b, z + 1, ag_up).start()

            @pl.when(within(c) & (z + k <= last))
            def _():
                b = z + k
                ag_copy(c, b, z, ag_dn).wait_recv()

                @pl.when(z > 0)
                def _():
                    ag_copy(c, b, z - 1, ag_dn).start()

        ce = t - base

        @pl.when(within(ce))
        def _():
            got = combined(ce, L - 1)
            for h in (0, 1):
                at = pl.ds(h * half, half)
                cols = pl.ds(pl.multiple_of(ce * w, w), w)
                hidden = got[h] * (1.0 / math.sqrt(1 << L))
                gate = ga_ref[at, cols].astype(F32)
                upper = ua_ref[at, cols].astype(F32)
                logistic = jax.nn.sigmoid(gate)
                scaled = hidden * logistic
                grads[ce, z, at, pl.ds(0, w)] = (
                    scaled * upper * (1.0 + gate * (1.0 - logistic))).astype(BF16)
                grads[ce, z, at, pl.ds(w, w)] = (scaled * gate).astype(BF16)

            @pl.when(z < last)
            def _():
                ag_copy(ce, z, z + 1, ag_up).start()

            @pl.when(z > 0)
            def _():
                ag_copy(ce, z, z - 1, ag_dn).start()

        for l in range(L - 1, 0, -1):
            cm = t - last - l

            @pl.when(within(cm))
            def _(l=l, cm=cm):
                got = combined(cm, l - 1)
                for h in (0, 1):
                    at = pl.ds(h * half, half)
                    cur[l, at, :] = got[h]
                    msend[l - 1, at, :] = got[h].astype(BF16)
                    mix_copy(cm, l, h).start()

        co = t - last

        @pl.when(within(co))
        def _():
            cur[0] = part[co % Z, z]

            @pl.when(z > 0)
            def _():
                rs_copy(co, z + 1, z).wait_recv()
                cur[0] += rs[co, z + 1].astype(F32)

            @pl.when(z < last)
            def _():
                rs_copy(co, z, z).wait_recv()
                cur[0] += rs[co, z].astype(F32)

            for h in (0, 1):
                mix_copy(co, 0, h).start()

        cu = t - z

        @pl.when(within(cu))
        def _():
            for b in range(Z - 1, 0, -1):
                @pl.when((b > z) & (z > 0))
                def _(b=b):
                    rs_copy(cu, b + 1, z).wait_recv()
                    rs[cu, b + 1] = (rs[cu, b + 1].astype(F32) + part[cu % Z, b]).astype(BF16)

                @pl.when((b > z) & (z == 0))
                def _(b=b):
                    rs[cu, b + 1] = part[cu % Z, b].astype(BF16)

                @pl.when(b > z)
                def _(b=b):
                    rs_copy(cu, b + 1, z + 1).start()

        cd = t - (last - z)

        @pl.when(within(cd))
        def _():
            for b in range(0, Z - 1):
                @pl.when((b < z) & (z < last))
                def _(b=b):
                    rs_copy(cd, b, z).wait_recv()
                    rs[cd, b] = (rs[cd, b].astype(F32) + part[cd % Z, b]).astype(BF16)

                @pl.when((b < z) & (z == last))
                def _(b=b):
                    rs[cd, b] = part[cd % Z, b].astype(BF16)

                @pl.when(b < z)
                def _(b=b):
                    rs_copy(cd, b, z - 1).start()

        c2 = t - base - last

        @pl.when(within(c2))
        def _():
            gw_fetch(c2).wait()
            uw_fetch(c2).wait()

            @pl.when(c2 + 1 < N)
            def _():
                gw_fetch(c2 + 1).start()
                uw_fetch(c2 + 1).start()

            width = acc.shape[1]
            tile = min(512, width)

            @pl.loop(0, Z)
            def _(b):
                at = pl.ds(pl.multiple_of(b * rows, rows), rows)
                for n in range(width // tile):
                    cols = pl.ds(n * tile, tile)
                    acc[at, cols] += dot_rows(grads[c2, b], wb[c2 % 2, cols, :])

        @pl.when(t + 1 < N)
        def _():
            @pl.when(t + 2 < N)
            def _():
                dw_fetch(t + 2).start()

            product(t + 1)

    @pl.loop(0, N)
    def _(c):
        for b in range(Z):
            @pl.when(b > z)
            def _():
                rs_copy(c, b + 1, z).wait_send()

            @pl.when(b < z)
            def _():
                rs_copy(c, b, z).wait_send()

            @pl.when((b <= z) & (z < last))
            def _():
                ag_copy(c, b, z, ag_up).wait_send()

            @pl.when((b >= z) & (z > 0))
            def _():
                ag_copy(c, b, z, ag_dn).wait_send()


def mixed_products(gathered, gate_act, up_act, gate_weight, up_weight, down_weight):
    Z, hids = lax.axis_size("tok"), lax.axis_size("hid")
    L = hids.bit_length() - 1
    rows, hidden = gate_act.shape
    w = 256 if hidden % 256 == 0 else 128
    N = hidden // w
    tokens, depth = gathered.shape
    vmem, hbm = pl.BlockSpec(memory_space=pltpu.VMEM), pl.BlockSpec(memory_space=pl.ANY)
    dma = pltpu.SemaphoreType.DMA
    flops = 6 * tokens * depth * hidden
    return pl.pallas_call(
        functools.partial(kernel, Z, L, N, w, rows),
        out_shape=jax.ShapeDtypeStruct((tokens, depth), F32),
        in_specs=[vmem, vmem, vmem, hbm, hbm, hbm],
        out_specs=vmem,
        scratch_shapes=[
            pltpu.VMEM((Z, Z, rows, w), F32),
            pltpu.VMEM((N, Z + 1, rows, w), BF16),
            pltpu.VMEM((N, rows, w), F32),
            pltpu.VMEM((N, L - 1, rows, w), BF16),
            pltpu.VMEM((L, rows, w), F32),
            pltpu.VMEM((L - 1, rows, w), BF16),
            pltpu.VMEM((N, Z, rows, 2 * w), BF16),
            pltpu.VMEM((2, w, depth), BF16),
            pltpu.VMEM((2, depth, 2 * w), BF16),
            dma((N, Z + 1)), dma((N, Z + 1)),
            dma((L, 2)), dma((N, L, 2)),
            dma((N, Z)), dma((N, Z)), dma((N, Z)),
            dma((2,)), dma((2,)), dma((2,)),
        ],
        compiler_params=pltpu.CompilerParams(
            collective_id=0, has_side_effects=True, vmem_limit_bytes=63 * 1024 * 1024),
        cost_estimate=pl.CostEstimate(
            flops=flops, bytes_accessed=6 * hidden * depth, transcendentals=rows * hidden),
    )(gathered, gate_act, up_act, gate_weight, up_weight, down_weight)


def body(out_grad, gate_act, up_act, gate_weight, up_weight, down_weight):
    gathered = lax.all_gather(out_grad, "hid", axis=0, tiled=True)
    total = mixed_products(gathered, gate_act, up_act, gate_weight, up_weight, down_weight)
    summed = lax.psum_scatter(total, "hid", scatter_dimension=0, tiled=True)
    return summed.astype(BF16)


def solution(mesh):
    in_specs = (
        P("hid", "tok"),
        P("tok", "hid"),
        P("tok", "hid"),
        P("tok", "hid"),
        P("tok", "hid"),
        P("hid", "tok"),
    )
    out_specs = P("hid", "tok")
    return jax.shard_map(body, mesh=mesh, in_specs=in_specs, out_specs=out_specs, check_vma=False)
```

```python
import functools
import math

import jax
import jax.numpy as jnp
from jax import lax
from jax.experimental import pallas as pl
from jax.experimental.pallas import tpu as pltpu
from jax.sharding import PartitionSpec as P

BF16, F32 = jnp.bfloat16, jnp.float32
MESH = pl.DeviceIdType.MESH


def subsets(items):
    found = [()]
    for item in items:
        found += [one + (item,) for one in found]
    return found


def dot_rows(left, right):
    return lax.dot_general(left, right, (((1,), (1,)), ((), ())), preferred_element_type=F32)


def kernel(
    Z, L, N, w, rows,
    x_hbm, ga_ref, ua_ref, gw_hbm, uw_hbm, dw_hbm, out_ref,
    xbuf, acc, stage, part, rs, mix0, mixn, cur, msend, grads, dwb, wb,
    rs_send, rs_recv, mix_send, mix_recv, ag_up, ag_dn, ag_recv, dw_sem, gw_sem, uw_sem,
    own_sem, head_send, head_recv, tail_send, tail_recv,
):
    z = lax.axis_index("tok")
    hid = lax.axis_index("hid")
    last = Z - 1
    half = rows // 2
    base = last + L
    steps = N + base + last
    order = [list(range(L)), [0] + list(range(L - 1, 0, -1))]
    head_order = [list(range(1, L)) + [0], list(range(L - 1, 0, -1)) + [0]]
    block, width = x_hbm.shape
    side = [pl.ds(h * (width // 2), width // 2) for h in (0, 1)]

    def bit_of(bit):
        return (hid // (1 << bit)) % 2

    def partner_of(bit):
        return hid + (1 - 2 * bit_of(bit)) * (1 << bit)

    def rows_of(p):
        return pl.ds(pl.multiple_of(p * block, block), block)

    def flipped(bits):
        return hid + sum((1 - 2 * bit_of(bit)) * (1 << bit) for bit in bits)

    def remote(src, dst, send, recv, **where):
        return pltpu.make_async_remote_copy(
            src_ref=src, dst_ref=dst, send_sem=send, recv_sem=recv,
            device_id=where, device_id_type=MESH,
        )

    def rs_copy(c, slot, to):
        return remote(rs.at[c, slot], rs.at[c, slot], rs_send.at[c, slot], rs_recv.at[c, slot], tok=to)

    def mix_copy(c, l, h):
        at = pl.ds(h * half, half)
        to = partner_of(order[h][l])
        if l == 0:
            src, dst = cur.at[0, at], mix0.at[c, at]
        else:
            src, dst = msend.at[l - 1, at], mixn.at[c, l - 1, at]
        return remote(src, dst, mix_send.at[l, h], mix_recv.at[c, l, h], hid=to)

    def ag_copy(c, b, to, sems):
        return remote(grads.at[c, b], grads.at[c, b], sems.at[c, b], ag_recv.at[c, b], tok=to)

    def head_copies(h, s, arriving):
        bit = head_order[h][s]
        copies = []
        for i, sub in enumerate(subsets(head_order[h][:s])):
            idx = (1 << s) - 1 + i
            at = xbuf.at[rows_of(flipped(sub + (bit,) if arriving else sub)), side[h]]
            copies.append(remote(
                at, at, head_send.at[h, idx], head_recv.at[h, idx], hid=partner_of(bit)))
        return copies

    def tail_steps(h, s):
        bit, rest = order[h][s], order[h][s + 1:]
        offset = (1 << L) - (1 << (L - s))
        found = []
        for i, sub in enumerate(subsets(rest)):
            idx = offset + i
            at = pl.ds(idx * block, block)
            copy = remote(
                stage.at[at, side[h]], xbuf.at[at, side[h]],
                tail_send.at[h, idx], tail_recv.at[h, idx], hid=partner_of(bit))
            found.append((flipped(sub), flipped(sub + (bit,)), at, copy))
        return found

    def dw_fetch(c):
        return pltpu.make_async_copy(
            dw_hbm.at[pl.ds(pl.multiple_of(c * w, w), w)], dwb.at[c % 2], dw_sem.at[c % 2])

    def gw_fetch(c):
        at = pl.ds(pl.multiple_of(c * w, w), w)
        return pltpu.make_async_copy(gw_hbm.at[:, at], wb.at[c % 2, :, pl.ds(0, w)], gw_sem.at[c % 2])

    def uw_fetch(c):
        at = pl.ds(pl.multiple_of(c * w, w), w)
        return pltpu.make_async_copy(uw_hbm.at[:, at], wb.at[c % 2, :, pl.ds(w, w)], uw_sem.at[c % 2])

    def within(c):
        return (c >= 0) & (c < N)

    def product(c):
        dw_fetch(c).wait()

        @pl.loop(0, Z)
        def _(b):
            at = pl.ds(pl.multiple_of(b * rows, rows), rows)
            part[c % Z, b] = dot_rows(xbuf[at, :], dwb[c % 2])

    barrier = pltpu.get_barrier_semaphore()

    @pl.when(z > 0)
    def _():
        pl.semaphore_signal(barrier, inc=1, device_id={"tok": z - 1}, device_id_type=MESH)

    @pl.when(z < last)
    def _():
        pl.semaphore_signal(barrier, inc=1, device_id={"tok": z + 1}, device_id_type=MESH)

    for bit in range(L):
        pl.semaphore_signal(barrier, inc=1, device_id={"hid": partner_of(bit)}, device_id_type=MESH)
    own = pltpu.make_async_copy(x_hbm, xbuf.at[rows_of(hid)], own_sem)
    own.start()
    dw_fetch(0).start()
    dw_fetch(1).start()
    gw_fetch(0).start()
    uw_fetch(0).start()
    pl.semaphore_wait(barrier, L + jnp.where(z > 0, 1, 0) + jnp.where(z < last, 1, 0))

    own.wait()
    for s in range(L):
        for h in (0, 1):
            if s > 0:
                for copy in head_copies(h, s - 1, True):
                    copy.wait_recv()
            for copy in head_copies(h, s, False):
                copy.start()
    acc[...] = jnp.zeros_like(acc)
    for h in (0, 1):
        for copy in head_copies(h, L - 1, True):
            copy.wait_recv()
    for s in range(L):
        for h in (0, 1):
            for copy in head_copies(h, s, False):
                copy.wait_send()
    product(0)

    def combined(c, l):
        halves = []
        for h in (0, 1):
            copy = mix_copy(c, l, h)
            copy.wait_send()
            copy.wait_recv()
            at = pl.ds(h * half, half)
            got = mix0[c, at, :] if l == 0 else mixn[c, l - 1, at, :].astype(F32)
            sign = jnp.where(bit_of(order[h][l]) == 1, -1.0, 1.0).astype(F32)
            halves.append(cur[l, at, :] * sign + got)
        return halves

    @pl.loop(0, steps)
    def _(t):
        for k in range(last, 0, -1):
            c = t - base - k

            @pl.when(within(c) & (z - k >= 0))
            def _():
                b = z - k
                ag_copy(c, b, z, ag_up).wait_recv()

                @pl.when(z < last)
                def _():
                    ag_copy(c, b, z + 1, ag_up).start()

            @pl.when(within(c) & (z + k <= last))
            def _():
                b = z + k
                ag_copy(c, b, z, ag_dn).wait_recv()

                @pl.when(z > 0)
                def _():
                    ag_copy(c, b, z - 1, ag_dn).start()

        ce = t - base

        @pl.when(within(ce))
        def _():
            got = combined(ce, L - 1)
            for h in (0, 1):
                at = pl.ds(h * half, half)
                cols = pl.ds(pl.multiple_of(ce * w, w), w)
                hidden = got[h] * (1.0 / math.sqrt(1 << L))
                gate = ga_ref[at, cols].astype(F32)
                upper = ua_ref[at, cols].astype(F32)
                logistic = jax.nn.sigmoid(gate)
                scaled = hidden * logistic
                grads[ce, z, at, pl.ds(0, w)] = (
                    scaled * upper * (1.0 + gate * (1.0 - logistic))).astype(BF16)
                grads[ce, z, at, pl.ds(w, w)] = (scaled * gate).astype(BF16)

            @pl.when(z < last)
            def _():
                ag_copy(ce, z, z + 1, ag_up).start()

            @pl.when(z > 0)
            def _():
                ag_copy(ce, z, z - 1, ag_dn).start()

        for l in range(L - 1, 0, -1):
            cm = t - last - l

            @pl.when(within(cm))
            def _(l=l, cm=cm):
                got = combined(cm, l - 1)
                for h in (0, 1):
                    at = pl.ds(h * half, half)
                    cur[l, at, :] = got[h]
                    msend[l - 1, at, :] = got[h].astype(BF16)
                    mix_copy(cm, l, h).start()

        co = t - last

        @pl.when(within(co))
        def _():
            cur[0] = part[co % Z, z]

            @pl.when(z > 0)
            def _():
                rs_copy(co, z + 1, z).wait_recv()
                cur[0] += rs[co, z + 1].astype(F32)

            @pl.when(z < last)
            def _():
                rs_copy(co, z, z).wait_recv()
                cur[0] += rs[co, z].astype(F32)

            for h in (0, 1):
                mix_copy(co, 0, h).start()

        cu = t - z

        @pl.when(within(cu))
        def _():
            for b in range(Z - 1, 0, -1):
                @pl.when((b > z) & (z > 0))
                def _(b=b):
                    rs_copy(cu, b + 1, z).wait_recv()
                    rs[cu, b + 1] = (rs[cu, b + 1].astype(F32) + part[cu % Z, b]).astype(BF16)

                @pl.when((b > z) & (z == 0))
                def _(b=b):
                    rs[cu, b + 1] = part[cu % Z, b].astype(BF16)

                @pl.when(b > z)
                def _(b=b):
                    rs_copy(cu, b + 1, z + 1).start()

        cd = t - (last - z)

        @pl.when(within(cd))
        def _():
            for b in range(0, Z - 1):
                @pl.when((b < z) & (z < last))
                def _(b=b):
                    rs_copy(cd, b, z).wait_recv()
                    rs[cd, b] = (rs[cd, b].astype(F32) + part[cd % Z, b]).astype(BF16)

                @pl.when((b < z) & (z == last))
                def _(b=b):
                    rs[cd, b] = part[cd % Z, b].astype(BF16)

                @pl.when(b < z)
                def _(b=b):
                    rs_copy(cd, b, z - 1).start()

        c2 = t - base - last

        @pl.when(within(c2))
        def _():
            gw_fetch(c2).wait()
            uw_fetch(c2).wait()

            @pl.when(c2 + 1 < N)
            def _():
                gw_fetch(c2 + 1).start()
                uw_fetch(c2 + 1).start()

            tile = min(512, width)

            @pl.loop(0, Z)
            def _(b):
                at = pl.ds(pl.multiple_of(b * rows, rows), rows)
                for n in range(width // tile):
                    cols = pl.ds(n * tile, tile)
                    acc[at, cols] += dot_rows(grads[c2, b], wb[c2 % 2, cols, :])

        @pl.when(t + 1 < N)
        def _():
            @pl.when(t + 2 < N)
            def _():
                dw_fetch(t + 2).start()

            product(t + 1)

    def add_arrived(h, s):
        for kept, _, at, copy in tail_steps(h, s):
            copy.wait_recv()
            acc[rows_of(kept), side[h]] += xbuf[at, side[h]].astype(F32)

    for s in range(L):
        for h in (0, 1):
            if s > 0:
                add_arrived(h, s - 1)
            for _, sent, at, copy in tail_steps(h, s):
                stage[at, side[h]] = acc[rows_of(sent), side[h]].astype(BF16)
                copy.start()
    for h in (0, 1):
        add_arrived(h, L - 1)
        out_ref[:, side[h]] = acc[rows_of(hid), side[h]].astype(BF16)
    for s in range(L):
        for h in (0, 1):
            for _, _, _, copy in tail_steps(h, s):
                copy.wait_send()

    @pl.loop(0, N)
    def _(c):
        for b in range(Z):
            @pl.when(b > z)
            def _():
                rs_copy(c, b + 1, z).wait_send()

            @pl.when(b < z)
            def _():
                rs_copy(c, b, z).wait_send()

            @pl.when((b <= z) & (z < last))
            def _():
                ag_copy(c, b, z, ag_up).wait_send()

            @pl.when((b >= z) & (z > 0))
            def _():
                ag_copy(c, b, z, ag_dn).wait_send()


def body(out_grad, gate_act, up_act, gate_weight, up_weight, down_weight):
    Z, hids = lax.axis_size("tok"), lax.axis_size("hid")
    L = hids.bit_length() - 1
    rows, hidden = gate_act.shape
    w = 256 if hidden % 256 == 0 else 128
    N = hidden // w
    block, depth = out_grad.shape
    tokens = hids * block
    vmem, hbm = pl.BlockSpec(memory_space=pltpu.VMEM), pl.BlockSpec(memory_space=pl.ANY)
    dma = pltpu.SemaphoreType.DMA
    flops = 6 * tokens * depth * hidden
    return pl.pallas_call(
        functools.partial(kernel, Z, L, N, w, rows),
        out_shape=jax.ShapeDtypeStruct((block, depth), BF16),
        in_specs=[hbm, vmem, vmem, hbm, hbm, hbm],
        out_specs=vmem,
        scratch_shapes=[
            pltpu.VMEM((tokens, depth), BF16),
            pltpu.VMEM((tokens, depth), F32),
            pltpu.VMEM((tokens - block, depth), BF16),
            pltpu.VMEM((Z, Z, rows, w), F32),
            pltpu.VMEM((N, Z + 1, rows, w), BF16),
            pltpu.VMEM((N, rows, w), F32),
            pltpu.VMEM((N, L - 1, rows, w), BF16),
            pltpu.VMEM((L, rows, w), F32),
            pltpu.VMEM((L - 1, rows, w), BF16),
            pltpu.VMEM((N, Z, rows, 2 * w), BF16),
            pltpu.VMEM((2, w, depth), BF16),
            pltpu.VMEM((2, depth, 2 * w), BF16),
            dma((N, Z + 1)), dma((N, Z + 1)),
            dma((L, 2)), dma((N, L, 2)),
            dma((N, Z)), dma((N, Z)), dma((N, Z)),
            dma((2,)), dma((2,)), dma((2,)),
            dma, dma((2, hids)), dma((2, hids)), dma((2, hids)), dma((2, hids)),
        ],
        compiler_params=pltpu.CompilerParams(
            collective_id=0, has_side_effects=True, vmem_limit_bytes=63 * 1024 * 1024),
        cost_estimate=pl.CostEstimate(
            flops=flops, bytes_accessed=6 * hidden * depth, transcendentals=rows * hidden),
    )(out_grad, gate_act, up_act, gate_weight, up_weight, down_weight)


def solution(mesh):
    in_specs = (
        P("hid", "tok"),
        P("tok", "hid"),
        P("tok", "hid"),
        P("tok", "hid"),
        P("tok", "hid"),
        P("hid", "tok"),
    )
    out_specs = P("hid", "tok")
    return jax.shard_map(body, mesh=mesh, in_specs=in_specs, out_specs=out_specs, check_vma=False)
```

```python
import functools
import math

import jax
import jax.numpy as jnp
from jax import lax
from jax.experimental import pallas as pl
from jax.experimental.pallas import tpu as pltpu
from jax.sharding import PartitionSpec as P

BF16, F32 = jnp.bfloat16, jnp.float32
MESH = pl.DeviceIdType.MESH


def subsets(items):
    found = [()]
    for item in items:
        found += [one + (item,) for one in found]
    return found


def dot_rows(left, right):
    return lax.dot_general(left, right, (((1,), (1,)), ((), ())), preferred_element_type=F32)


def kernel(
    Z, L, N, w, rows,
    x_hbm, ga_ref, ua_ref, gw_hbm, uw_hbm, dw_hbm, out_ref,
    xbuf, acc, stage, part, rs, mix0, mixn, cur, msend, grads, dwb, wb,
    rs_send, rs_recv, mix_send, mix_recv, ag_up, ag_dn, ag_recv, dw_sem, gw_sem, uw_sem,
    own_sem, head_send, head_recv, tail_send, tail_recv,
):
    z = lax.axis_index("tok")
    hid = lax.axis_index("hid")
    last = Z - 1
    half = rows // 2
    base = last + L
    steps = N + base + last
    order = [list(range(L)), [0] + list(range(L - 1, 0, -1))]
    head_order = [list(range(1, L)) + [0], list(range(L - 1, 0, -1)) + [0]]
    block, width = x_hbm.shape
    side = [pl.ds(h * (width // 2), width // 2) for h in (0, 1)]

    def bit_of(bit):
        return (hid // (1 << bit)) % 2

    def partner_of(bit):
        return hid + (1 - 2 * bit_of(bit)) * (1 << bit)

    def rows_of(p):
        return pl.ds(pl.multiple_of(p * block, block), block)

    def flipped(bits):
        return hid + sum((1 - 2 * bit_of(bit)) * (1 << bit) for bit in bits)

    def remote(src, dst, send, recv, **where):
        return pltpu.make_async_remote_copy(
            src_ref=src, dst_ref=dst, send_sem=send, recv_sem=recv,
            device_id=where, device_id_type=MESH,
        )

    def rs_copy(c, slot, to):
        return remote(rs.at[c, slot], rs.at[c, slot], rs_send.at[c, slot], rs_recv.at[c, slot], tok=to)

    def mix_copy(c, l, h):
        at = pl.ds(h * half, half)
        to = partner_of(order[h][l])
        if l == 0:
            src, dst = cur.at[0, at], mix0.at[c, at]
        else:
            src, dst = msend.at[l - 1, at], mixn.at[c, l - 1, at]
        return remote(src, dst, mix_send.at[l, h], mix_recv.at[c, l, h], hid=to)

    def ag_copy(c, b, to, sems):
        return remote(grads.at[c, b], grads.at[c, b], sems.at[c, b], ag_recv.at[c, b], tok=to)

    def head_copies(h, s, arriving):
        bit = head_order[h][s]
        copies = []
        for i, sub in enumerate(subsets(head_order[h][:s])):
            idx = (1 << s) - 1 + i
            at = xbuf.at[rows_of(flipped(sub + (bit,) if arriving else sub)), side[h]]
            copies.append(remote(
                at, at, head_send.at[h, idx], head_recv.at[h, idx], hid=partner_of(bit)))
        return copies

    def tail_steps(h, s):
        bit, rest = order[h][s], order[h][s + 1:]
        offset = (1 << L) - (1 << (L - s))
        found = []
        for i, sub in enumerate(subsets(rest)):
            idx = offset + i
            at = pl.ds(idx * block, block)
            copy = remote(
                stage.at[at, side[h]], xbuf.at[at, side[h]],
                tail_send.at[h, idx], tail_recv.at[h, idx], hid=partner_of(bit))
            found.append((flipped(sub), flipped(sub + (bit,)), at, copy))
        return found

    def dw_fetch(c):
        return pltpu.make_async_copy(
            dw_hbm.at[pl.ds(pl.multiple_of(c * w, w), w)], dwb.at[c % 2], dw_sem.at[c % 2])

    def gw_fetch(c):
        at = pl.ds(pl.multiple_of(c * w, w), w)
        return pltpu.make_async_copy(gw_hbm.at[:, at], wb.at[c % 2, :, pl.ds(0, w)], gw_sem.at[c % 2])

    def uw_fetch(c):
        at = pl.ds(pl.multiple_of(c * w, w), w)
        return pltpu.make_async_copy(uw_hbm.at[:, at], wb.at[c % 2, :, pl.ds(w, w)], uw_sem.at[c % 2])

    def within(c):
        return (c >= 0) & (c < N)

    def product(c):
        dw_fetch(c).wait()

        @pl.loop(0, Z)
        def _(b):
            at = pl.ds(pl.multiple_of(b * rows, rows), rows)
            part[c % Z, b] = dot_rows(xbuf[at, :], dwb[c % 2])

    barrier = pltpu.get_barrier_semaphore()

    @pl.when(z > 0)
    def _():
        pl.semaphore_signal(barrier, inc=1, device_id={"tok": z - 1}, device_id_type=MESH)

    @pl.when(z < last)
    def _():
        pl.semaphore_signal(barrier, inc=1, device_id={"tok": z + 1}, device_id_type=MESH)

    for bit in range(L):
        pl.semaphore_signal(barrier, inc=1, device_id={"hid": partner_of(bit)}, device_id_type=MESH)
    own = pltpu.make_async_copy(x_hbm, xbuf.at[rows_of(hid)], own_sem)
    own.start()
    dw_fetch(0).start()
    dw_fetch(1).start()
    gw_fetch(0).start()
    uw_fetch(0).start()
    pl.semaphore_wait(barrier, L + jnp.where(z > 0, 1, 0) + jnp.where(z < last, 1, 0))

    own.wait()
    for s in range(L):
        for h in (0, 1):
            if s > 0:
                for copy in head_copies(h, s - 1, True):
                    copy.wait_recv()
            for copy in head_copies(h, s, False):
                copy.start()
    acc[...] = jnp.zeros_like(acc)
    for h in (0, 1):
        for copy in head_copies(h, L - 1, True):
            copy.wait_recv()
    for s in range(L):
        for h in (0, 1):
            for copy in head_copies(h, s, False):
                copy.wait_send()
    product(0)

    def combined(c, l):
        halves = []
        for h in (0, 1):
            copy = mix_copy(c, l, h)
            copy.wait_send()
            copy.wait_recv()
            at = pl.ds(h * half, half)
            got = mix0[c, at, :] if l == 0 else mixn[c, l - 1, at, :].astype(F32)
            sign = jnp.where(bit_of(order[h][l]) == 1, -1.0, 1.0).astype(F32)
            halves.append(cur[l, at, :] * sign + got)
        return halves

    @pl.loop(0, steps)
    def _(t):
        for k in range(last, 0, -1):
            c = t - base - k

            @pl.when(within(c) & (z - k >= 0))
            def _():
                b = z - k
                ag_copy(c, b, z, ag_up).wait_recv()

                @pl.when(z < last)
                def _():
                    ag_copy(c, b, z + 1, ag_up).start()

            @pl.when(within(c) & (z + k <= last))
            def _():
                b = z + k
                ag_copy(c, b, z, ag_dn).wait_recv()

                @pl.when(z > 0)
                def _():
                    ag_copy(c, b, z - 1, ag_dn).start()

        ce = t - base

        @pl.when(within(ce))
        def _():
            got = combined(ce, L - 1)
            for h in (0, 1):
                at = pl.ds(h * half, half)
                cols = pl.ds(pl.multiple_of(ce * w, w), w)
                hidden = got[h] * (1.0 / math.sqrt(1 << L))
                gate = ga_ref[at, cols].astype(F32)
                upper = ua_ref[at, cols].astype(F32)
                logistic = jax.nn.sigmoid(gate)
                scaled = hidden * logistic
                grads[ce, z, at, pl.ds(0, w)] = (
                    scaled * upper * (1.0 + gate * (1.0 - logistic))).astype(BF16)
                grads[ce, z, at, pl.ds(w, w)] = (scaled * gate).astype(BF16)

            @pl.when(z < last)
            def _():
                ag_copy(ce, z, z + 1, ag_up).start()

            @pl.when(z > 0)
            def _():
                ag_copy(ce, z, z - 1, ag_dn).start()

        for l in range(L - 1, 0, -1):
            cm = t - last - l

            @pl.when(within(cm))
            def _(l=l, cm=cm):
                got = combined(cm, l - 1)
                for h in (0, 1):
                    at = pl.ds(h * half, half)
                    cur[l, at, :] = got[h]
                    msend[l - 1, at, :] = got[h].astype(BF16)
                    mix_copy(cm, l, h).start()

        co = t - last

        @pl.when(within(co))
        def _():
            cur[0] = part[co % Z, z]

            @pl.when(z > 0)
            def _():
                rs_copy(co, z + 1, z).wait_recv()
                cur[0] += rs[co, z + 1].astype(F32)

            @pl.when(z < last)
            def _():
                rs_copy(co, z, z).wait_recv()
                cur[0] += rs[co, z].astype(F32)

            for h in (0, 1):
                mix_copy(co, 0, h).start()

        cu = t - z

        @pl.when(within(cu))
        def _():
            for b in range(Z - 1, 0, -1):
                @pl.when((b > z) & (z > 0))
                def _(b=b):
                    rs_copy(cu, b + 1, z).wait_recv()
                    rs[cu, b + 1] = (rs[cu, b + 1].astype(F32) + part[cu % Z, b]).astype(BF16)

                @pl.when((b > z) & (z == 0))
                def _(b=b):
                    rs[cu, b + 1] = part[cu % Z, b].astype(BF16)

                @pl.when(b > z)
                def _(b=b):
                    rs_copy(cu, b + 1, z + 1).start()

        cd = t - (last - z)

        @pl.when(within(cd))
        def _():
            for b in range(0, Z - 1):
                @pl.when((b < z) & (z < last))
                def _(b=b):
                    rs_copy(cd, b, z).wait_recv()
                    rs[cd, b] = (rs[cd, b].astype(F32) + part[cd % Z, b]).astype(BF16)

                @pl.when((b < z) & (z == last))
                def _(b=b):
                    rs[cd, b] = part[cd % Z, b].astype(BF16)

                @pl.when(b < z)
                def _(b=b):
                    rs_copy(cd, b, z - 1).start()

        c2 = t - base - last

        @pl.when(within(c2))
        def _():
            gw_fetch(c2).wait()
            uw_fetch(c2).wait()

            @pl.when(c2 + 1 < N)
            def _():
                gw_fetch(c2 + 1).start()
                uw_fetch(c2 + 1).start()

            tile = min(512, width)

            @pl.loop(0, Z)
            def _(b):
                at = pl.ds(pl.multiple_of(b * rows, rows), rows)
                for n in range(width // tile):
                    cols = pl.ds(n * tile, tile)
                    acc[at, cols] += dot_rows(grads[c2, b], wb[c2 % 2, cols, :])

        @pl.when(t + 1 < N)
        def _():
            @pl.when(t + 2 < N)
            def _():
                dw_fetch(t + 2).start()

            product(t + 1)

    def add_arrived(h, s):
        for kept, _, at, copy in tail_steps(h, s):
            copy.wait_recv()
            acc[rows_of(kept), side[h]] += xbuf[at, side[h]].astype(F32)

    for s in range(L):
        for h in (0, 1):
            if s > 0:
                add_arrived(h, s - 1)
            for _, sent, at, copy in tail_steps(h, s):
                stage[at, side[h]] = acc[rows_of(sent), side[h]].astype(BF16)
                copy.start()
    for h in (0, 1):
        add_arrived(h, L - 1)
        out_ref[:, side[h]] = acc[rows_of(hid), side[h]].astype(BF16)
    for s in range(L):
        for h in (0, 1):
            for _, _, _, copy in tail_steps(h, s):
                copy.wait_send()

    @pl.loop(0, N)
    def _(c):
        for b in range(Z):
            @pl.when(b > z)
            def _():
                rs_copy(c, b + 1, z).wait_send()

            @pl.when(b < z)
            def _():
                rs_copy(c, b, z).wait_send()

            @pl.when((b <= z) & (z < last))
            def _():
                ag_copy(c, b, z, ag_up).wait_send()

            @pl.when((b >= z) & (z > 0))
            def _():
                ag_copy(c, b, z, ag_dn).wait_send()


def body(out_grad, gate_act, up_act, gate_weight, up_weight, down_weight):
    Z, hids = lax.axis_size("tok"), lax.axis_size("hid")
    L = hids.bit_length() - 1
    rows, hidden = gate_act.shape
    w = 128
    N = hidden // w
    block, depth = out_grad.shape
    tokens = hids * block
    vmem, hbm = pl.BlockSpec(memory_space=pltpu.VMEM), pl.BlockSpec(memory_space=pl.ANY)
    dma = pltpu.SemaphoreType.DMA
    flops = 6 * tokens * depth * hidden
    return pl.pallas_call(
        functools.partial(kernel, Z, L, N, w, rows),
        out_shape=jax.ShapeDtypeStruct((block, depth), BF16),
        in_specs=[hbm, vmem, vmem, hbm, hbm, hbm],
        out_specs=vmem,
        scratch_shapes=[
            pltpu.VMEM((tokens, depth), BF16),
            pltpu.VMEM((tokens, depth), F32),
            pltpu.VMEM((tokens - block, depth), BF16),
            pltpu.VMEM((Z, Z, rows, w), F32),
            pltpu.VMEM((N, Z + 1, rows, w), BF16),
            pltpu.VMEM((N, rows, w), F32),
            pltpu.VMEM((N, L - 1, rows, w), BF16),
            pltpu.VMEM((L, rows, w), F32),
            pltpu.VMEM((L - 1, rows, w), BF16),
            pltpu.VMEM((N, Z, rows, 2 * w), BF16),
            pltpu.VMEM((2, w, depth), BF16),
            pltpu.VMEM((2, depth, 2 * w), BF16),
            dma((N, Z + 1)), dma((N, Z + 1)),
            dma((L, 2)), dma((N, L, 2)),
            dma((N, Z)), dma((N, Z)), dma((N, Z)),
            dma((2,)), dma((2,)), dma((2,)),
            dma, dma((2, hids)), dma((2, hids)), dma((2, hids)), dma((2, hids)),
        ],
        compiler_params=pltpu.CompilerParams(
            collective_id=0, has_side_effects=True, vmem_limit_bytes=63 * 1024 * 1024),
        cost_estimate=pl.CostEstimate(
            flops=flops, bytes_accessed=6 * hidden * depth, transcendentals=rows * hidden),
    )(out_grad, gate_act, up_act, gate_weight, up_weight, down_weight)


def solution(mesh):
    in_specs = (
        P("hid", "tok"),
        P("tok", "hid"),
        P("tok", "hid"),
        P("tok", "hid"),
        P("tok", "hid"),
        P("hid", "tok"),
    )
    out_specs = P("hid", "tok")
    return jax.shard_map(body, mesh=mesh, in_specs=in_specs, out_specs=out_specs, check_vma=False)
```
